32 devices in a mesh: groups: 2 (over y), blk: 8 (over z, x), rhs: 2 (over core).
Axes of the slice: x: 2, y: 2, z: 4, core: 2. Of those that a mesh axis runs over, the one named last changes fastest.
Arguments:
- forward: bfloat16 [128, 32, 256], P(('groups', 'blk'), 'rhs'), parts along dimension 0, may hold values from -6 to 6
- adjoint: bfloat16 [128, 32, 256], P(('groups', 'blk'), 'rhs'), parts along dimension 0, may hold values from -6 to 6
- row_home: int32 [128], P('groups'), parts along dimension 0, may hold values from 0 to 63, as said below
- block_rows: int32 [2, 512], P(None, ('groups', 'blk')), parts along dimension 1, may hold values from 0 to 63, as said below
- block_cols: int32 [2, 512], P(None, ('groups', 'blk')), parts along dimension 1, may hold values from 0 to 63, as said below
Outputs:
- grads: bfloat16 [2, 512, 256, 256], P(None, ('groups', 'blk'), 'rhs'), parts along dimension 1
The draws below stay inside these ranges and needn't reach their ends.
There are 2 independent parts, one for each index of `groups`. The reference program is written for one: setup_inputs(seed, part) draws one part's arguments, and reference() takes and returns one part's arrays. A program takes and returns all parts, laid end to end along the dimension named above; each array names one. Nothing has to cross between parts.
Inputs may be any that keep to these rules, and one draw needn't show every extreme that they name: `row_home`: a permutation: each slot holds exactly one row block; the slot's holder along blk is its slot // 8. `block_rows`: within one device's entries of both strips together (64), at most 8 name row blocks held by any one device, and exactly 8 for some holder. `block_cols`: within one device's entries of both strips together (64), at most 8 name row blocks held by any one device, and exactly 8 for some holder.
All inputs are finite; a program needn't handle non-finite values.
Results may differ from the reference program's by a relative error of at most 0.001.
Values may be sent and summed in bfloat16 or wider, within the bound.
No kernel may reach another device: no remote copies, remote signals or barrier semaphores. Data moves between devices by JAX's collectives and lax.ppermute only.
A program may use at most 64 MiB of HBM per device.

```python
from functools import partial
import jax
import jax.numpy as jnp
from jax import lax

BLOCK = 256
RB_DEV = 8
NZ_DEV = 32
NB = 64
RHS = 32
N_BLK = 8


def shared_home(key):
    return jax.random.permutation(key, NB).astype(jnp.int32)


def strip_pattern(key, held):
    entries = 2 * NZ_DEV

    def one_list(subkey):
        first, second, third = jax.random.split(subkey, 3)
        ranking = jax.random.permutation(first, N_BLK)
        capacity = (entries + N_BLK - 1) // N_BLK
        owner = ranking[jnp.arange(entries) // capacity]
        owner = owner[jax.random.permutation(second, entries)]
        local = jax.random.randint(third, (entries,), 0, RB_DEV)
        return held[owner * RB_DEV + local]
    key_list = jax.random.split(key, N_BLK)
    blocks = jax.vmap(one_list)(key_list).reshape(N_BLK, 2, NZ_DEV)
    blocks = jnp.transpose(blocks, (1, 0, 2))
    return blocks.reshape(2, NZ_DEV * N_BLK).astype(jnp.int32)


def draw_row_home(key, part):
    home = shared_home(key)
    return home


def draw_block_rows(key, part):
    home = shared_home(key)
    held = jnp.argsort(home, stable=True)
    key = jax.random.fold_in(key, 11)
    return strip_pattern(key, held)


def draw_block_cols(key, part):
    home = shared_home(key)
    held = jnp.argsort(home, stable=True)
    key = jax.random.fold_in(key, 12)
    return strip_pattern(key, held)


def block_levels(rng, dims, pieces, least, top_value):
    factor_of = 1.0
    for position, parts in pieces:
        steps = jax.random.uniform(jax.random.fold_in(jax.random.fold_in(rng, 6), position), (parts,), jnp.float32, least / len(pieces), top_value / len(pieces))
        factor_of = factor_of * jnp.repeat(jnp.exp(steps), dims[position] // parts).reshape((-1,) + (1,) * (len(dims) - 1 - position))
    return factor_of


def scatter_about(rng, extent, spread, bound, shards=(), kind=jnp.bfloat16):
    values = jax.random.normal(rng, extent, jnp.float32) * spread
    if len(shards) > 0:
        values = block_levels(rng, extent, shards, -0.22, 0.18) * values
    return jnp.clip(values, min=-bound, max=bound).astype(kind)


def setup_inputs(seed: int = 0, part: int = 0) -> dict:
    key_of = jax.random.split(jax.random.key(seed), 6)
    part_keys = jax.random.split(jax.random.fold_in(key_of[5], part), 6)
    return {
        "forward": scatter_about(part_keys[0], (NB, RHS, BLOCK), 1.0, 6.0, ((0, 8), (1, 2))),
        "adjoint": scatter_about(part_keys[1], (NB, RHS, BLOCK), 1.0, 6.0, ((0, 8), (1, 2))),
        "row_home": draw_row_home(jax.random.fold_in(jax.random.fold_in(key_of[5], part), 71), part),
        "block_rows": draw_block_rows(jax.random.fold_in(jax.random.fold_in(key_of[5], part), 71), part),
        "block_cols": draw_block_cols(jax.random.fold_in(jax.random.fold_in(key_of[5], part), 71), part),
    }


def grad_blocks(forward, adjoint, row_home, pair):
    row_ids, col_ids = pair
    left = jnp.take(adjoint, row_home[row_ids], axis=0).astype(jnp.float32)
    right = jnp.take(forward, row_home[col_ids], axis=0).astype(jnp.float32)
    return (-jnp.einsum("kra,krb->kab", left, right)).astype(jnp.bfloat16)


def reference(forward, adjoint, row_home, block_rows, block_cols):
    group_size = 64
    total = block_rows.shape[1]
    rows_flat = block_rows.reshape(-1, group_size)
    cols_flat = block_cols.reshape(-1, group_size)
    result = lax.map(partial(grad_blocks, forward, adjoint, row_home), (rows_flat, cols_flat))
    return result.reshape(2, total, BLOCK, BLOCK)
```

```python
import functools

import jax
import jax.numpy as jnp
from jax import lax
from jax.experimental import pallas as pl
from jax.experimental.pallas import tpu as pltpu
from jax.sharding import PartitionSpec as P

STEP = 8
ANY = pl.BlockSpec(memory_space=pl.ANY)
SMEM = pl.BlockSpec(memory_space=pltpu.SMEM)
VMEM = pl.BlockSpec(memory_space=pltpu.VMEM)


def placing(blocks, row_home, stored, owners, capacity):
    slot_of = jnp.take(row_home, blocks)
    owner = slot_of // stored
    local = slot_of % stored
    order = jnp.arange(blocks.shape[0])
    earlier = (owner[:, None] == owner[None, :]) & (order[None, :] < order[:, None])
    rank = jnp.sum(earlier.astype(jnp.int32), axis=1)
    place = owner * capacity + rank
    targets = jnp.arange(owners * capacity)
    table = jnp.sum(jnp.where(place[:, None] == targets[None, :], local[:, None], 0), axis=0)
    return (table.reshape(owners, capacity), place)


def fetch(row_table, col_table, left_source, right_source):
    left = jnp.take(
        left_source,
        lax.all_to_all(row_table, "blk", split_axis=0, concat_axis=0, tiled=True),
        axis=0,
    )
    right = jnp.take(
        right_source,
        lax.all_to_all(col_table, "blk", split_axis=0, concat_axis=0, tiled=True),
        axis=0,
    )
    return (
        lax.all_to_all(left, "blk", split_axis=0, concat_axis=0, tiled=True),
        lax.all_to_all(right, "blk", split_axis=0, concat_axis=0, tiled=True),
    )


def select(fetched, place):
    flat = fetched.reshape((-1,) + fetched.shape[2:])
    return jnp.take(flat, place, axis=0)


def finish(left, right, half_start, half_width):
    left, right = (
        lax.all_gather(left, "rhs", axis=1, tiled=True),
        lax.all_gather(right, "rhs", axis=1, tiled=True),
    )
    left = lax.dynamic_slice_in_dim(left, half_start, half_width, 2)
    product = jnp.einsum("kra,krb->kab", left, right, preferred_element_type=jnp.float32)
    return (-product).astype(jnp.bfloat16)


def tabled(forward, adjoint, row_home, block_rows, block_cols):
    owners = lax.axis_size("blk")
    stored = forward.shape[0]
    slot_count = block_rows.shape[1]
    capacity = (2 * slot_count + owners - 1) // owners
    width = forward.shape[2]
    half_width = width // 2
    half_start = lax.axis_index("rhs") * half_width
    left_source, right_source = (adjoint, forward)
    row_table, row_place = placing(block_rows.reshape(-1), row_home, stored, owners, capacity)
    col_table, col_place = placing(block_cols.reshape(-1), row_home, stored, owners, capacity)
    left_all, right_all = fetch(row_table, col_table, left_source, right_source)
    result = finish(
        select(left_all, row_place), select(right_all, col_place), half_start, half_width
    )
    return result.reshape(2, slot_count, half_width, width)


def join_kernel(a, b, out, sem):
    n = a.shape[0]
    copies = [
        pltpu.make_async_copy(a, out.at[pl.ds(0, n)], sem.at[0]),
        pltpu.make_async_copy(b, out.at[pl.ds(n, n)], sem.at[1]),
    ]
    for copy in copies:
        copy.start()
    for copy in copies:
        copy.wait()


def join(a, b):
    return pl.pallas_call(
        join_kernel,
        out_shape=pltpu.VMEM((2 * a.shape[0],) + a.shape[1:], a.dtype),
        in_specs=[ANY, ANY],
        out_specs=ANY,
        scratch_shapes=[pltpu.SemaphoreType.DMA((2,))],
        compiler_params=pltpu.CompilerParams(vmem_limit_bytes=1 << 20),
    )(*(pltpu.with_memory_space_constraint(v, pltpu.HBM) for v in (a, b)))


def products_kernel(owners, stored, half, *refs):
    mine, others = refs[:owners], refs[owners : 2 * owners]
    home, rows, cols, out = refs[2 * owners : 2 * owners + 4]
    home_s, rows_s, cols_s, left, right, result, in_sem, index_sem, out_sem = refs[2 * owners + 4 :]
    start = pl.multiple_of(lax.axis_index("rhs") * half, half)
    me = lax.axis_index("blk")
    rhs = mine[0].shape[1]
    copies = [
        pltpu.make_async_copy(home, home_s, index_sem.at[0]),
        pltpu.make_async_copy(rows, rows_s, index_sem.at[1]),
        pltpu.make_async_copy(cols, cols_s, index_sem.at[2]),
    ]
    for j in range(owners):
        slots = pl.ds(j * stored, stored)
        for c, source in enumerate((mine[j], others[j])):
            part = pl.ds(c * rhs, rhs)
            copies.append(
                pltpu.make_async_copy(
                    source.at[pl.ds(0, stored)], right.at[slots, part], in_sem.at[c, 0, j]
                )
            )
            copies.append(
                pltpu.make_async_copy(
                    source.at[pl.ds(stored, stored), :, pl.ds(start, half)],
                    left.at[slots, part],
                    in_sem.at[c, 1, j],
                )
            )
    for copy in copies:
        copy.start()
    for copy in copies:
        copy.wait()

    _, per_strip = rows_s.shape
    steps = result.shape[0] // STEP

    def place(block):
        slot = home_s[block]
        owner = lax.div(slot, stored)
        return jnp.bitwise_xor(owner, me) * stored + lax.rem(slot, stored)

    def out_copy(step):
        part = pl.ds(step * STEP, STEP)
        return pltpu.make_async_copy(result.at[part], out.at[part], out_sem.at[step])

    def one_step(step, carry):
        strip, first = lax.div(step * STEP, per_strip), lax.rem(step * STEP, per_strip)
        for k in range(STEP):
            a = left[place(rows_s[strip, first + k])]
            b = right[place(cols_s[strip, first + k])]
            product = lax.dot_general(
                -a, b, (((0,), (0,)), ((), ())), preferred_element_type=jnp.float32
            )
            result[step * STEP + k] = product.astype(jnp.bfloat16)
        out_copy(step).start()
        return carry

    lax.fori_loop(0, steps, one_step, 0)

    def drain(step, carry):
        out_copy(step).wait()
        return carry

    lax.fori_loop(0, steps, drain, 0)


def products(mine, others, row_home, block_rows, block_cols):
    owners = len(mine)
    joined, rhs, width = mine[0].shape
    stored, half = joined // 2, width // 2
    entries = block_rows.size
    index = [
        pltpu.with_memory_space_constraint(v, pltpu.HBM)
        for v in (row_home, block_rows, block_cols)
    ]
    return pl.pallas_call(
        functools.partial(products_kernel, owners, stored, half),
        out_shape=jax.ShapeDtypeStruct((entries, half, width), jnp.bfloat16),
        in_specs=[ANY] * (2 * owners + 3),
        out_specs=ANY,
        scratch_shapes=[
            pltpu.SMEM(row_home.shape, jnp.int32),
            pltpu.SMEM(block_rows.shape, jnp.int32),
            pltpu.SMEM(block_cols.shape, jnp.int32),
            pltpu.VMEM((owners * stored, 2 * rhs, half), jnp.bfloat16),
            pltpu.VMEM((owners * stored, 2 * rhs, width), jnp.bfloat16),
            pltpu.VMEM((entries, half, width), jnp.bfloat16),
            pltpu.SemaphoreType.DMA((2, 2, owners)),
            pltpu.SemaphoreType.DMA((3,)),
            pltpu.SemaphoreType.DMA((entries // STEP,)),
        ],
        compiler_params=pltpu.CompilerParams(vmem_limit_bytes=24 << 20),
    )(*mine, *others, *index)


PLAN = ((4, 4), (3, 3), (2, 2), (1, 1), (7, 3), (6, 2), (5, 1))


def gathered(forward, adjoint, row_home, block_rows, block_cols):
    owners = lax.axis_size("blk")

    def across(value, mask):
        return lax.ppermute(value, "blk", [(i, i ^ mask) for i in range(owners)])

    held = {0: join(forward, adjoint)}
    for mask, via in PLAN:
        held[mask] = across(held[mask ^ via], via)
    mine = [held[j] for j in range(owners)]
    others = [lax.ppermute(v, "rhs", [(0, 1), (1, 0)]) for v in mine]
    result = products(mine, others, row_home, block_rows, block_cols)
    return result.reshape(2, block_rows.shape[1], *result.shape[1:])


def body(forward, adjoint, row_home, block_rows, block_cols):
    if lax.axis_size("blk") == 8 and forward.shape[0] * 8 <= 2 * block_rows.shape[1]:
        return gathered(forward, adjoint, row_home, block_rows, block_cols)
    return tabled(forward, adjoint, row_home, block_rows, block_cols)


def solution(mesh):
    placed = (
        P(("groups", "blk"), "rhs", None),
        P(("groups", "blk"), "rhs", None),
        P("groups"),
        P(None, ("groups", "blk")),
        P(None, ("groups", "blk")),
    )
    return jax.shard_map(
        body,
        mesh=mesh,
        in_specs=placed,
        out_specs=P(None, ("groups", "blk"), "rhs", None),
        check_vma=False,
    )
```

```python
import functools

import jax
import jax.numpy as jnp
from jax import lax
from jax.experimental import pallas as pl
from jax.experimental.pallas import tpu as pltpu
from jax.sharding import PartitionSpec as P

CHUNK = 4
ANY = pl.BlockSpec(memory_space=pl.ANY)
SMEM = pl.BlockSpec(memory_space=pltpu.SMEM)
VMEM = pl.BlockSpec(memory_space=pltpu.VMEM)


def placing(blocks, row_home, stored, owners, capacity):
    slot_of = jnp.take(row_home, blocks)
    owner = slot_of // stored
    local = slot_of % stored
    order = jnp.arange(blocks.shape[0])
    earlier = (owner[:, None] == owner[None, :]) & (order[None, :] < order[:, None])
    rank = jnp.sum(earlier.astype(jnp.int32), axis=1)
    place = owner * capacity + rank
    targets = jnp.arange(owners * capacity)
    table = jnp.sum(jnp.where(place[:, None] == targets[None, :], local[:, None], 0), axis=0)
    return (table.reshape(owners, capacity), place)


def fetch(row_table, col_table, left_source, right_source):
    left = jnp.take(
        left_source,
        lax.all_to_all(row_table, "blk", split_axis=0, concat_axis=0, tiled=True),
        axis=0,
    )
    right = jnp.take(
        right_source,
        lax.all_to_all(col_table, "blk", split_axis=0, concat_axis=0, tiled=True),
        axis=0,
    )
    return (
        lax.all_to_all(left, "blk", split_axis=0, concat_axis=0, tiled=True),
        lax.all_to_all(right, "blk", split_axis=0, concat_axis=0, tiled=True),
    )


def select(fetched, place):
    flat = fetched.reshape((-1,) + fetched.shape[2:])
    return jnp.take(flat, place, axis=0)


def finish(left, right, half_start, half_width):
    left, right = (
        lax.all_gather(left, "rhs", axis=1, tiled=True),
        lax.all_gather(right, "rhs", axis=1, tiled=True),
    )
    left = lax.dynamic_slice_in_dim(left, half_start, half_width, 2)
    product = jnp.einsum("kra,krb->kab", left, right, preferred_element_type=jnp.float32)
    return (-product).astype(jnp.bfloat16)


def tabled(forward, adjoint, row_home, block_rows, block_cols):
    owners = lax.axis_size("blk")
    stored = forward.shape[0]
    slot_count = block_rows.shape[1]
    capacity = (2 * slot_count + owners - 1) // owners
    width = forward.shape[2]
    half_width = width // 2
    half_start = lax.axis_index("rhs") * half_width
    left_source, right_source = (adjoint, forward)
    row_table, row_place = placing(block_rows.reshape(-1), row_home, stored, owners, capacity)
    col_table, col_place = placing(block_cols.reshape(-1), row_home, stored, owners, capacity)
    left_all, right_all = fetch(row_table, col_table, left_source, right_source)
    result = finish(
        select(left_all, row_place), select(right_all, col_place), half_start, half_width
    )
    return result.reshape(2, slot_count, half_width, width)


def load_kernel(a, b, home, rows, cols, out, home_s, rows_s, cols_s, sem):
    n = a.shape[0]
    pairs = (
        (a, out.at[pl.ds(0, n)]),
        (b, out.at[pl.ds(n, n)]),
        (home, home_s),
        (rows, rows_s),
        (cols, cols_s),
    )
    copies = [pltpu.make_async_copy(*pair, sem.at[k]) for k, pair in enumerate(pairs)]
    for copy in copies:
        copy.start()
    for copy in copies:
        copy.wait()


def load(a, b, index):
    return pl.pallas_call(
        load_kernel,
        out_shape=[pltpu.VMEM((2 * a.shape[0],) + a.shape[1:], a.dtype)]
        + [pltpu.SMEM(v.shape, v.dtype) for v in index],
        in_specs=[ANY] * 5,
        out_specs=[VMEM] + [SMEM] * 3,
        scratch_shapes=[pltpu.SemaphoreType.DMA((5,))],
        compiler_params=pltpu.CompilerParams(vmem_limit_bytes=1 << 20),
    )(*(pltpu.with_memory_space_constraint(v, pltpu.HBM) for v in (a, b) + index))


def stage(shards, left, right):
    joined, rhs, _ = shards[0].shape
    stored, half = joined // 2, left.shape[2]
    start = pl.multiple_of(lax.axis_index("rhs") * half, half)
    for n, shard in enumerate(shards):
        slots = slice(n // 2 * stored, (n // 2 + 1) * stored)
        part = slice(n % 2 * rhs, (n % 2 + 1) * rhs)
        right[slots, part] = shard[:stored]
        left[slots, part] = -shard[stored:, :, pl.ds(start, half)]


def products_kernel(stored, *refs):
    shards, refs = refs[:-8], refs[-8:]
    home, rows, cols, out, left, right, result, sem = refs
    stage(shards, left, right)
    mine = lax.axis_index("blk") * stored
    strips, per_strip = rows.shape
    chunks = strips * per_strip // CHUNK

    def out_copy(n):
        part = pl.ds(n * CHUNK, CHUNK)
        return pltpu.make_async_copy(result.at[part], out.at[part], sem.at[n])

    def one_strip(strip, carry):
        for k in range(per_strip):
            a = left[jnp.bitwise_xor(home[rows[strip, k]], mine)]
            b = right[jnp.bitwise_xor(home[cols[strip, k]], mine)]
            product = lax.dot_general(
                a, b, (((0,), (0,)), ((), ())), preferred_element_type=jnp.float32
            )
            result[strip * per_strip + k] = product.astype(jnp.bfloat16)
            if k % CHUNK == CHUNK - 1:
                out_copy(strip * (per_strip // CHUNK) + k // CHUNK).start()
        return carry

    lax.fori_loop(0, strips, one_strip, 0)

    def drain(n, carry):
        out_copy(n).wait()
        return carry

    lax.fori_loop(0, chunks, drain, 0)


def products(shards, index):
    joined, rhs, width = shards[0].shape
    stored, half = joined // 2, width // 2
    slots = len(shards) // 2 * stored
    entries = index[1].size
    out = jax.ShapeDtypeStruct((entries, half, width), jnp.bfloat16)
    return pl.pallas_call(
        functools.partial(products_kernel, stored),
        out_shape=out,
        in_specs=[VMEM] * len(shards) + [SMEM] * 3,
        out_specs=ANY,
        scratch_shapes=[
            pltpu.VMEM((slots, 2 * rhs, half), jnp.bfloat16),
            pltpu.VMEM((slots, 2 * rhs, width), jnp.bfloat16),
            pltpu.VMEM(out.shape, out.dtype),
            pltpu.SemaphoreType.DMA((entries // CHUNK,)),
        ],
        compiler_params=pltpu.CompilerParams(vmem_limit_bytes=16 << 20),
    )(*shards, *index)


PLAN = ((4, 4), (3, 3), (2, 2), (1, 1), (7, 3), (6, 2), (5, 1))


def gathered(forward, adjoint, row_home, block_rows, block_cols):
    owners = lax.axis_size("blk")

    def across(value, mask):
        return lax.ppermute(value, "blk", [(i, i ^ mask) for i in range(owners)])

    own, *index = load(forward, adjoint, (row_home, block_rows, block_cols))
    held = {0: own}
    for mask, via in PLAN:
        held[mask] = across(held[mask ^ via], via)
    shards = []
    for j in range(owners):
        shards += [held[j], lax.ppermute(held[j], "rhs", [(0, 1), (1, 0)])]
    result = products(shards, index)
    return result.reshape(2, block_rows.shape[1], *result.shape[1:])


def body(forward, adjoint, row_home, block_rows, block_cols):
    owners, stored = lax.axis_size("blk"), forward.shape[0]
    few = owners * stored <= 2 * block_rows.shape[1]
    if few and owners == 8 and stored & (stored - 1) == 0 and block_rows.shape[1] % CHUNK == 0:
        return gathered(forward, adjoint, row_home, block_rows, block_cols)
    return tabled(forward, adjoint, row_home, block_rows, block_cols)


def solution(mesh):
    placed = (
        P(("groups", "blk"), "rhs", None),
        P(("groups", "blk"), "rhs", None),
        P("groups"),
        P(None, ("groups", "blk")),
        P(None, ("groups", "blk")),
    )
    return jax.shard_map(
        body,
        mesh=mesh,
        in_specs=placed,
        out_specs=P(None, ("groups", "blk"), "rhs", None),
        check_vma=False,
    )
```

```python
import functools

import jax
import jax.numpy as jnp
from jax import lax
from jax.experimental import pallas as pl
from jax.experimental.pallas import tpu as pltpu
from jax.sharding import PartitionSpec as P

CHUNK = 4
ANY = pl.BlockSpec(memory_space=pl.ANY)
SMEM = pl.BlockSpec(memory_space=pltpu.SMEM)
VMEM = pl.BlockSpec(memory_space=pltpu.VMEM)


def placing(blocks, row_home, stored, owners, capacity):
    slot_of = jnp.take(row_home, blocks)
    owner = slot_of // stored
    local = slot_of % stored
    order = jnp.arange(blocks.shape[0])
    earlier = (owner[:, None] == owner[None, :]) & (order[None, :] < order[:, None])
    rank = jnp.sum(earlier.astype(jnp.int32), axis=1)
    place = owner * capacity + rank
    targets = jnp.arange(owners * capacity)
    table = jnp.sum(jnp.where(place[:, None] == targets[None, :], local[:, None], 0), axis=0)
    return (table.reshape(owners, capacity), place)


def fetch(row_table, col_table, left_source, right_source):
    left = jnp.take(
        left_source,
        lax.all_to_all(row_table, "blk", split_axis=0, concat_axis=0, tiled=True),
        axis=0,
    )
    right = jnp.take(
        right_source,
        lax.all_to_all(col_table, "blk", split_axis=0, concat_axis=0, tiled=True),
        axis=0,
    )
    return (
        lax.all_to_all(left, "blk", split_axis=0, concat_axis=0, tiled=True),
        lax.all_to_all(right, "blk", split_axis=0, concat_axis=0, tiled=True),
    )


def select(fetched, place):
    flat = fetched.reshape((-1,) + fetched.shape[2:])
    return jnp.take(flat, place, axis=0)


def finish(left, right, half_start, half_width):
    left, right = (
        lax.all_gather(left, "rhs", axis=1, tiled=True),
        lax.all_gather(right, "rhs", axis=1, tiled=True),
    )
    left = lax.dynamic_slice_in_dim(left, half_start, half_width, 2)
    product = jnp.einsum("kra,krb->kab", left, right, preferred_element_type=jnp.float32)
    return (-product).astype(jnp.bfloat16)


def tabled(forward, adjoint, row_home, block_rows, block_cols):
    owners = lax.axis_size("blk")
    stored = forward.shape[0]
    slot_count = block_rows.shape[1]
    capacity = (2 * slot_count + owners - 1) // owners
    width = forward.shape[2]
    half_width = width // 2
    half_start = lax.axis_index("rhs") * half_width
    left_source, right_source = (adjoint, forward)
    row_table, row_place = placing(block_rows.reshape(-1), row_home, stored, owners, capacity)
    col_table, col_place = placing(block_cols.reshape(-1), row_home, stored, owners, capacity)
    left_all, right_all = fetch(row_table, col_table, left_source, right_source)
    result = finish(
        select(left_all, row_place), select(right_all, col_place), half_start, half_width
    )
    return result.reshape(2, slot_count, half_width, width)


def load_kernel(a, b, home, rows, cols, out, home_s, rows_s, cols_s, sem):
    n = a.shape[0]
    pairs = (
        (a, out.at[pl.ds(0, n)]),
        (b, out.at[pl.ds(n, n)]),
        (home, home_s),
        (rows, rows_s),
        (cols, cols_s),
    )
    copies = [pltpu.make_async_copy(*pair, sem.at[k]) for k, pair in enumerate(pairs)]
    for copy in copies:
        copy.start()
    for copy in copies:
        copy.wait()


def load(a, b, index):
    return pl.pallas_call(
        load_kernel,
        out_shape=[pltpu.VMEM((2 * a.shape[0],) + a.shape[1:], a.dtype)]
        + [pltpu.SMEM(v.shape, v.dtype) for v in index],
        in_specs=[ANY] * 5,
        out_specs=[VMEM] + [SMEM] * 3,
        scratch_shapes=[pltpu.SemaphoreType.DMA((5,))],
        compiler_params=pltpu.CompilerParams(vmem_limit_bytes=1 << 20),
    )(*(pltpu.with_memory_space_constraint(v, pltpu.HBM) for v in (a, b) + index))


def stage(shards, left, right):
    joined, rhs, _ = shards[0].shape
    stored, half = joined // 2, left.shape[2]
    start = pl.multiple_of(lax.axis_index("rhs") * half, half)
    for n, shard in enumerate(shards):
        slots = slice(n // 2 * stored, (n // 2 + 1) * stored)
        part = slice(n % 2 * rhs, (n % 2 + 1) * rhs)
        right[slots, part] = shard[:stored]
        left[slots, part] = -shard[stored:, :, pl.ds(start, half)]


def products_kernel(stored, *refs):
    shards, refs = refs[:-8], refs[-8:]
    home, rows, cols, out, left, right, result, sem = refs
    stage(shards, left, right)
    mine = lax.axis_index("blk") * stored
    strips, per_strip = rows.shape
    chunks = strips * per_strip // CHUNK

    def out_copy(n):
        part = pl.ds(n * CHUNK, CHUNK)
        return pltpu.make_async_copy(result.at[part], out.at[part], sem.at[n])

    def one_strip(strip, carry):
        for k in range(per_strip):
            a = left[jnp.bitwise_xor(home[rows[strip, k]], mine)]
            b = right[jnp.bitwise_xor(home[cols[strip, k]], mine)]
            product = lax.dot_general(
                a, b, (((0,), (0,)), ((), ())), preferred_element_type=jnp.float32
            )
            result[strip * per_strip + k] = product.astype(jnp.bfloat16)
            if k % CHUNK == CHUNK - 1:
                out_copy(strip * (per_strip // CHUNK) + k // CHUNK).start()
        return carry

    lax.fori_loop(0, strips, one_strip, 0)

    def drain(n, carry):
        out_copy(n).wait()
        return carry

    lax.fori_loop(0, chunks, drain, 0)


def products(shards, index):
    joined, rhs, width = shards[0].shape
    stored, half = joined // 2, width // 2
    slots = len(shards) // 2 * stored
    entries = index[1].size
    out = jax.ShapeDtypeStruct((entries, half, width), jnp.bfloat16)
    return pl.pallas_call(
        functools.partial(products_kernel, stored),
        out_shape=out,
        in_specs=[VMEM] * len(shards) + [SMEM] * 3,
        out_specs=ANY,
        scratch_shapes=[
            pltpu.VMEM((slots, 2 * rhs, half), jnp.bfloat16),
            pltpu.VMEM((slots, 2 * rhs, width), jnp.bfloat16),
            pltpu.VMEM(out.shape, out.dtype),
            pltpu.SemaphoreType.DMA((entries // CHUNK,)),
        ],
        compiler_params=pltpu.CompilerParams(vmem_limit_bytes=16 << 20),
    )(*shards, *index)


PLAN = ((6, 6), (2, 2), (1, 1), (3, 2), (7, 1), (4, 2), (5, 1))


def gathered(forward, adjoint, row_home, block_rows, block_cols):
    owners = lax.axis_size("blk")

    def across(value, mask):
        return lax.ppermute(value, "blk", [(i, i ^ mask) for i in range(owners)])

    own, *index = load(forward, adjoint, (row_home, block_rows, block_cols))
    held = {0: own}
    for mask, via in PLAN:
        held[mask] = across(held[mask ^ via], via)
    shards = []
    for j in range(owners):
        shards += [held[j], lax.ppermute(held[j], "rhs", [(0, 1), (1, 0)])]
    result = products(shards, index)
    return result.reshape(2, block_rows.shape[1], *result.shape[1:])


def body(forward, adjoint, row_home, block_rows, block_cols):
    owners, stored = lax.axis_size("blk"), forward.shape[0]
    few = owners * stored <= 2 * block_rows.shape[1]
    if few and owners == 8 and stored & (stored - 1) == 0 and block_rows.shape[1] % CHUNK == 0:
        return gathered(forward, adjoint, row_home, block_rows, block_cols)
    return tabled(forward, adjoint, row_home, block_rows, block_cols)


def solution(mesh):
    placed = (
        P(("groups", "blk"), "rhs", None),
        P(("groups", "blk"), "rhs", None),
        P("groups"),
        P(None, ("groups", "blk")),
        P(None, ("groups", "blk")),
    )
    return jax.shard_map(
        body,
        mesh=mesh,
        in_specs=placed,
        out_specs=P(None, ("groups", "blk"), "rhs", None),
        check_vma=False,
    )
```

```python
import functools

import jax
import jax.numpy as jnp
from jax import lax
from jax.experimental import pallas as pl
from jax.experimental.pallas import tpu as pltpu
from jax.sharding import PartitionSpec as P

CHUNK = 4
ANY = pl.BlockSpec(memory_space=pl.ANY)
SMEM = pl.BlockSpec(memory_space=pltpu.SMEM)
VMEM = pl.BlockSpec(memory_space=pltpu.VMEM)


def placing(blocks, row_home, stored, owners, capacity):
    slot_of = jnp.take(row_home, blocks)
    owner = slot_of // stored
    local = slot_of % stored
    order = jnp.arange(blocks.shape[0])
    earlier = (owner[:, None] == owner[None, :]) & (order[None, :] < order[:, None])
    rank = jnp.sum(earlier.astype(jnp.int32), axis=1)
    place = owner * capacity + rank
    targets = jnp.arange(owners * capacity)
    table = jnp.sum(jnp.where(place[:, None] == targets[None, :], local[:, None], 0), axis=0)
    return (table.reshape(owners, capacity), place)


def fetch(row_table, col_table, left_source, right_source):
    left = jnp.take(
        left_source,
        lax.all_to_all(row_table, "blk", split_axis=0, concat_axis=0, tiled=True),
        axis=0,
    )
    right = jnp.take(
        right_source,
        lax.all_to_all(col_table, "blk", split_axis=0, concat_axis=0, tiled=True),
        axis=0,
    )
    return (
        lax.all_to_all(left, "blk", split_axis=0, concat_axis=0, tiled=True),
        lax.all_to_all(right, "blk", split_axis=0, concat_axis=0, tiled=True),
    )


def select(fetched, place):
    flat = fetched.reshape((-1,) + fetched.shape[2:])
    return jnp.take(flat, place, axis=0)


def finish(left, right, half_start, half_width):
    left, right = (
        lax.all_gather(left, "rhs", axis=1, tiled=True),
        lax.all_gather(right, "rhs", axis=1, tiled=True),
    )
    left = lax.dynamic_slice_in_dim(left, half_start, half_width, 2)
    product = jnp.einsum("kra,krb->kab", left, right, preferred_element_type=jnp.float32)
    return (-product).astype(jnp.bfloat16)


def tabled(forward, adjoint, row_home, block_rows, block_cols):
    owners = lax.axis_size("blk")
    stored = forward.shape[0]
    slot_count = block_rows.shape[1]
    capacity = (2 * slot_count + owners - 1) // owners
    width = forward.shape[2]
    half_width = width // 2
    half_start = lax.axis_index("rhs") * half_width
    left_source, right_source = (adjoint, forward)
    row_table, row_place = placing(block_rows.reshape(-1), row_home, stored, owners, capacity)
    col_table, col_place = placing(block_cols.reshape(-1), row_home, stored, owners, capacity)
    left_all, right_all = fetch(row_table, col_table, left_source, right_source)
    result = finish(
        select(left_all, row_place), select(right_all, col_place), half_start, half_width
    )
    return result.reshape(2, slot_count, half_width, width)


def load_kernel(a, b, home, rows, cols, out, home_s, rows_s, cols_s, sem):
    n = a.shape[0]
    pairs = (
        (a, out.at[pl.ds(0, n)]),
        (b, out.at[pl.ds(n, n)]),
        (home, home_s),
        (rows, rows_s),
        (cols, cols_s),
    )
    copies = [pltpu.make_async_copy(*pair, sem.at[k]) for k, pair in enumerate(pairs)]
    for copy in copies:
        copy.start()
    for copy in copies:
        copy.wait()


def load(a, b, index):
    return pl.pallas_call(
        load_kernel,
        out_shape=[pltpu.VMEM((2 * a.shape[0],) + a.shape[1:], a.dtype)]
        + [pltpu.SMEM(v.shape, v.dtype) for v in index],
        in_specs=[ANY] * 5,
        out_specs=[VMEM] + [SMEM] * 3,
        scratch_shapes=[pltpu.SemaphoreType.DMA((5,))],
        compiler_params=pltpu.CompilerParams(vmem_limit_bytes=1 << 20),
    )(*(pltpu.with_memory_space_constraint(v, pltpu.HBM) for v in (a, b) + index))


def stage(shards, left, right):
    joined, rhs, _ = shards[0].shape
    stored, half = joined // 2, left.shape[2]
    start = pl.multiple_of(lax.axis_index("rhs") * half, half)
    for n, shard in enumerate(shards):
        slots = slice(n // 2 * stored, (n // 2 + 1) * stored)
        part = slice(n % 2 * rhs, (n % 2 + 1) * rhs)
        right[slots, part] = shard[:stored]
        left[slots, part] = -shard[stored:, :, pl.ds(start, half)]


def products_kernel(stored, *refs):
    shards, refs = refs[:-8], refs[-8:]
    home, rows, cols, out, left, right, result, sem = refs
    stage(shards, left, right)
    mine = lax.axis_index("blk") * stored
    strips, per_strip = rows.shape
    chunks = strips * per_strip // CHUNK

    def out_copy(n):
        part = pl.ds(n * CHUNK, CHUNK)
        return pltpu.make_async_copy(result.at[part], out.at[part], sem.at[n])

    def one_strip(strip, carry):
        for k in range(per_strip):
            a = left[jnp.bitwise_xor(home[rows[strip, k]], mine)]
            b = right[jnp.bitwise_xor(home[cols[strip, k]], mine)]
            product = lax.dot_general(
                a, b, (((0,), (0,)), ((), ())), preferred_element_type=jnp.float32
            )
            result[strip * per_strip + k] = product.astype(jnp.bfloat16)
            if k % CHUNK == CHUNK - 1:
                out_copy(strip * (per_strip // CHUNK) + k // CHUNK).start()
        return carry

    for strip in range(strips):
        one_strip(strip, 0)

    def drain(n, carry):
        out_copy(n).wait()
        return carry

    lax.fori_loop(0, chunks, drain, 0)


def products(shards, index):
    joined, rhs, width = shards[0].shape
    stored, half = joined // 2, width // 2
    slots = len(shards) // 2 * stored
    entries = index[1].size
    out = jax.ShapeDtypeStruct((entries, half, width), jnp.bfloat16)
    return pl.pallas_call(
        functools.partial(products_kernel, stored),
        out_shape=out,
        in_specs=[VMEM] * len(shards) + [SMEM] * 3,
        out_specs=ANY,
        scratch_shapes=[
            pltpu.VMEM((slots, 2 * rhs, half), jnp.bfloat16),
            pltpu.VMEM((slots, 2 * rhs, width), jnp.bfloat16),
            pltpu.VMEM(out.shape, out.dtype),
            pltpu.SemaphoreType.DMA((entries // CHUNK,)),
        ],
        compiler_params=pltpu.CompilerParams(vmem_limit_bytes=16 << 20),
    )(*shards, *index)


PLAN = ((6, 6), (2, 2), (1, 1), (3, 2), (7, 1), (4, 2), (5, 1))


def gathered(forward, adjoint, row_home, block_rows, block_cols):
    owners = lax.axis_size("blk")

    def across(value, mask):
        return lax.ppermute(value, "blk", [(i, i ^ mask) for i in range(owners)])

    own, *index = load(forward, adjoint, (row_home, block_rows, block_cols))
    held = {0: own}
    for mask, via in PLAN:
        held[mask] = across(held[mask ^ via], via)
    shards = []
    for j in range(owners):
        shards += [held[j], lax.ppermute(held[j], "rhs", [(0, 1), (1, 0)])]
    result = products(shards, index)
    return result.reshape(2, block_rows.shape[1], *result.shape[1:])


def body(forward, adjoint, row_home, block_rows, block_cols):
    owners, stored = lax.axis_size("blk"), forward.shape[0]
    few = owners * stored <= 2 * block_rows.shape[1]
    if few and owners == 8 and stored & (stored - 1) == 0 and block_rows.shape[1] % CHUNK == 0:
        return gathered(forward, adjoint, row_home, block_rows, block_cols)
    return tabled(forward, adjoint, row_home, block_rows, block_cols)


def solution(mesh):
    placed = (
        P(("groups", "blk"), "rhs", None),
        P(("groups", "blk"), "rhs", None),
        P("groups"),
        P(None, ("groups", "blk")),
        P(None, ("groups", "blk")),
    )
    return jax.shard_map(
        body,
        mesh=mesh,
        in_specs=placed,
        out_specs=P(None, ("groups", "blk"), "rhs", None),
        check_vma=False,
    )
```

```python
import functools

import jax
import jax.numpy as jnp
from jax import lax
from jax.experimental import pallas as pl
from jax.experimental.pallas import tpu as pltpu
from jax.sharding import PartitionSpec as P

CHUNK = 4
ANY = pl.BlockSpec(memory_space=pl.ANY)
SMEM = pl.BlockSpec(memory_space=pltpu.SMEM)
VMEM = pl.BlockSpec(memory_space=pltpu.VMEM)


def placing(blocks, row_home, stored, owners, capacity):
    slot_of = jnp.take(row_home, blocks)
    owner = slot_of // stored
    local = slot_of % stored
    order = jnp.arange(blocks.shape[0])
    earlier = (owner[:, None] == owner[None, :]) & (order[None, :] < order[:, None])
    rank = jnp.sum(earlier.astype(jnp.int32), axis=1)
    place = owner * capacity + rank
    targets = jnp.arange(owners * capacity)
    table = jnp.sum(jnp.where(place[:, None] == targets[None, :], local[:, None], 0), axis=0)
    return (table.reshape(owners, capacity), place)


def fetch(row_table, col_table, left_source, right_source):
    left = jnp.take(
        left_source,
        lax.all_to_all(row_table, "blk", split_axis=0, concat_axis=0, tiled=True),
        axis=0,
    )
    right = jnp.take(
        right_source,
        lax.all_to_all(col_table, "blk", split_axis=0, concat_axis=0, tiled=True),
        axis=0,
    )
    return (
        lax.all_to_all(left, "blk", split_axis=0, concat_axis=0, tiled=True),
        lax.all_to_all(right, "blk", split_axis=0, concat_axis=0, tiled=True),
    )


def select(fetched, place):
    flat = fetched.reshape((-1,) + fetched.shape[2:])
    return jnp.take(flat, place, axis=0)


def finish(left, right, half_start, half_width):
    left, right = (
        lax.all_gather(left, "rhs", axis=1, tiled=True),
        lax.all_gather(right, "rhs", axis=1, tiled=True),
    )
    left = lax.dynamic_slice_in_dim(left, half_start, half_width, 2)
    product = jnp.einsum("kra,krb->kab", left, right, preferred_element_type=jnp.float32)
    return (-product).astype(jnp.bfloat16)


def tabled(forward, adjoint, row_home, block_rows, block_cols):
    owners = lax.axis_size("blk")
    stored = forward.shape[0]
    slot_count = block_rows.shape[1]
    capacity = (2 * slot_count + owners - 1) // owners
    width = forward.shape[2]
    half_width = width // 2
    half_start = lax.axis_index("rhs") * half_width
    left_source, right_source = (adjoint, forward)
    row_table, row_place = placing(block_rows.reshape(-1), row_home, stored, owners, capacity)
    col_table, col_place = placing(block_cols.reshape(-1), row_home, stored, owners, capacity)
    left_all, right_all = fetch(row_table, col_table, left_source, right_source)
    result = finish(
        select(left_all, row_place), select(right_all, col_place), half_start, half_width
    )
    return result.reshape(2, slot_count, half_width, width)


def load_kernel(a, b, home, rows, cols, out, home_s, rows_s, cols_s, sem):
    n = a.shape[0]
    size = n // 2
    pairs = [(home, home_s), (rows, rows_s), (cols, cols_s)]
    for k in range(2):
        pairs.append((a.at[pl.ds(k * size, size)], out.at[pl.ds(k * size, size)]))
        pairs.append((b.at[pl.ds(k * size, size)], out.at[pl.ds(n + k * size, size)]))
    copies = [pltpu.make_async_copy(*pair, sem.at[k]) for k, pair in enumerate(pairs)]
    for copy in copies:
        copy.start()
    for copy in copies:
        copy.wait()


def load(a, b, index):
    return pl.pallas_call(
        load_kernel,
        out_shape=[pltpu.VMEM((2 * a.shape[0],) + a.shape[1:], a.dtype)]
        + [pltpu.SMEM(v.shape, v.dtype) for v in index],
        in_specs=[ANY] * 5,
        out_specs=[VMEM] + [SMEM] * 3,
        scratch_shapes=[pltpu.SemaphoreType.DMA((7,))],
        compiler_params=pltpu.CompilerParams(vmem_limit_bytes=1 << 20),
    )(*(pltpu.with_memory_space_constraint(v, pltpu.HBM) for v in (a, b) + index))


def stage(masks, shards, left, right):
    joined, rhs, _ = shards[0].shape
    stored, half = joined // 2, left.shape[2]
    core = lax.axis_index("rhs")
    start = pl.multiple_of(core * half, half)
    for n, shard in enumerate(shards):
        mine, other = masks[n // 2] if n % 2 == 0 else masks[n // 2][::-1]
        first = jnp.where(core == 0, mine, other) * stored
        part = slice(n % 2 * rhs, (n % 2 + 1) * rhs)
        right[pl.ds(first, stored), part] = shard[:stored]
        left[pl.ds(first, stored), part] = -shard[stored:, :, pl.ds(start, half)]


def products_kernel(stored, masks, *refs):
    shards, refs = refs[:-8], refs[-8:]
    home, rows, cols, out, left, right, result, sem = refs
    stage(masks, shards, left, right)
    mine = lax.axis_index("blk") * stored
    strips, per_strip = rows.shape
    chunks = strips * per_strip // CHUNK

    def out_copy(n):
        part = pl.ds(n * CHUNK, CHUNK)
        return pltpu.make_async_copy(result.at[part], out.at[part], sem.at[n])

    def one_strip(strip):
        for k in range(per_strip):
            a = left[jnp.bitwise_xor(home[rows[strip, k]], mine)]
            b = right[jnp.bitwise_xor(home[cols[strip, k]], mine)]
            product = lax.dot_general(
                a, b, (((0,), (0,)), ((), ())), preferred_element_type=jnp.float32
            )
            result[strip * per_strip + k] = product.astype(jnp.bfloat16)
            if k % CHUNK == CHUNK - 1:
                out_copy(strip * (per_strip // CHUNK) + k // CHUNK).start()

    for strip in range(strips):
        one_strip(strip)

    def drain(n, carry):
        out_copy(n).wait()
        return carry

    lax.fori_loop(0, chunks, drain, 0)


def products(masks, shards, index):
    joined, rhs, width = shards[0].shape
    stored, half = joined // 2, width // 2
    slots = len(shards) // 2 * stored
    entries = index[1].size
    out = jax.ShapeDtypeStruct((entries, half, width), jnp.bfloat16)
    return pl.pallas_call(
        functools.partial(products_kernel, stored, masks),
        out_shape=out,
        in_specs=[VMEM] * len(shards) + [SMEM] * 3,
        out_specs=ANY,
        scratch_shapes=[
            pltpu.VMEM((slots, 2 * rhs, half), jnp.bfloat16),
            pltpu.VMEM((slots, 2 * rhs, width), jnp.bfloat16),
            pltpu.VMEM(out.shape, out.dtype),
            pltpu.SemaphoreType.DMA((entries // CHUNK,)),
        ],
        compiler_params=pltpu.CompilerParams(vmem_limit_bytes=16 << 20),
    )(*shards, *index)


PLAN = ((0, 6, 4), (0, 2, 1), (0, 1, 2), (2, 1, 2), (1, 1, 2), (1, 2, 1), (5, 2, 1))


def gathered(forward, adjoint, row_home, block_rows, block_cols):
    owners = lax.axis_size("blk")

    def across(value, *steps):
        pairs = [(2 * i + c, 2 * (i ^ steps[c]) + c) for i in range(owners) for c in range(2)]
        return lax.ppermute(value, ("blk", "rhs"), pairs)

    own, *index = load(forward, adjoint, (row_home, block_rows, block_cols))
    held, masks = [own], [(0, 0)]
    for source, first, second in PLAN:
        held.append(across(held[source], first, second))
        masks.append((masks[source][0] ^ first, masks[source][1] ^ second))
    shards = []
    for v in held:
        shards += [v, lax.ppermute(v, "rhs", [(0, 1), (1, 0)])]
    result = products(masks, shards, index)
    return result.reshape(2, block_rows.shape[1], *result.shape[1:])


def body(forward, adjoint, row_home, block_rows, block_cols):
    owners, stored = lax.axis_size("blk"), forward.shape[0]
    few = owners * stored <= 2 * block_rows.shape[1]
    whole = owners == 8 and lax.axis_size("rhs") == 2 and stored & (stored - 1) == 0
    if few and whole and block_rows.shape[1] % CHUNK == 0:
        return gathered(forward, adjoint, row_home, block_rows, block_cols)
    return tabled(forward, adjoint, row_home, block_rows, block_cols)


def solution(mesh):
    placed = (
        P(("groups", "blk"), "rhs", None),
        P(("groups", "blk"), "rhs", None),
        P("groups"),
        P(None, ("groups", "blk")),
        P(None, ("groups", "blk")),
    )
    return jax.shard_map(
        body,
        mesh=mesh,
        in_specs=placed,
        out_specs=P(None, ("groups", "blk"), "rhs", None),
        check_vma=False,
    )
```
